256 devices in a mesh: expert: 32 (over x, z), tensor: 8 (over y, core).
Axes of the slice: x: 4, y: 4, z: 8, core: 2. Of those that a mesh axis runs over, the one named last changes fastest.
Arguments:
- tokens: bfloat16 [4096, 7168], P('expert', 'tensor'), may hold values from -6 to 6
- routes: int32 [4096, 8], P('expert'), may hold values from 0 to 31, all different within a row; in each aligned block of 128 rows (0 to 127, 128 to 255, ...) at most 40 rows name the same one
- gate_scales: float32 [4096, 8], P('expert'), may hold values from 0.1 to 0.5
- gate_weight: bfloat16 [32, 7168, 2048], P('expert', None, 'tensor'), may hold values from -0.0625 to 0.0625
- up_weight: bfloat16 [32, 7168, 2048], P('expert', None, 'tensor'), may hold values from -0.0625 to 0.0625
- down_weight: bfloat16 [32, 2048, 7168], P('expert', None, 'tensor'), may hold values from -0.125 to 0.125
Outputs:
- mixed: bfloat16 [4096, 7168], P('expert', 'tensor')
The draws below stay inside these ranges and needn't reach their ends.
Inputs may be any that keep to these rules, and one draw needn't show every extreme that they name: `routes`: within each block of 128 consecutive tokens (the tokens of one device), no expert is chosen by more than 40 of them, and in some block one expert is chosen by exactly 40. The 8 experts of a token are distinct, and every expert is chosen by some token.
All inputs are finite; a program needn't handle non-finite values.
Results may differ from the reference program's by a relative error of at most 0.0057.
Values may be sent and summed in bfloat16 or wider, within the bound.
No kernel may reach another device: no remote copies, remote signals or barrier semaphores. Data moves between devices by JAX's collectives and lax.ppermute only.
A program may use at most 128 MiB of HBM per device.

```python
import math
import jax
import jax.numpy as jnp
import numpy as np
from jax import lax

D = 7168
FF = 2048
TOP = 8
TOK_DEV = 128
EXPERTS = 32
CAP = 40
TOKENS = 4096


def level_of(rng, extent, cuts, least, largest):
    level = 1.0
    for position, parts in cuts:
        draws = jax.random.uniform(jax.random.fold_in(jax.random.fold_in(rng, 6), position), (parts,), jnp.float32, least / len(cuts), largest / len(cuts))
        level = level * jnp.repeat(jnp.exp(draws), extent[position] // parts).reshape((-1,) + (1,) * (len(extent) - 1 - position))
    return level


def routed_block(own_key, own, number, rows, number_of, top, limit, slope):
    order = jax.random.permutation(own_key, number_of)
    heavy_load, usual = shares(number_of, rows * top, limit, slope, True), shares(number_of, rows * top, limit, slope, False)
    places = jnp.arange(number_of)

    def named(sizes, rotation):
        used = int((sizes > 0).sum())
        fixed = max(1, used // 4)
        passed = fixed + (places - fixed + rotation * (used - fixed)) % max(1, number_of - fixed)
        return jnp.zeros((number_of,), jnp.int32).at[order[jnp.where(places < fixed, places, passed)]].set(jnp.asarray(sizes, jnp.int32))

    sizes = jnp.where(number % 4 == 0, named(heavy_load, number // 4), named(usual, number - number // 4 - 1))
    mixed = jax.random.permutation(jax.random.fold_in(own, 3), number_of)
    donor, taker = mixed[0:number_of // 2 * 2:2], mixed[1:number_of // 2 * 2:2]
    slack = jnp.minimum(sizes[donor] - 1, limit - sizes[taker]) // 2
    slack = jnp.where((donor == order[0]) | (taker == order[0]) | (sizes[taker] == 0), 0, jnp.maximum(slack, 0))
    passed = jax.random.randint(jax.random.fold_in(own, 4), (number_of // 2,), 0, 1 << 20) % (slack + 1)
    sizes = sizes.at[donor].add(-passed).at[taker].add(passed)
    items = jnp.searchsorted(jnp.cumsum(sizes), jnp.arange(rows * top), side="right").astype(jnp.int32)
    listing = items.reshape(top, rows).T
    listing = listing[jax.random.permutation(jax.random.fold_in(own, 1), rows)]
    rotation = jax.random.randint(jax.random.fold_in(own, 2), (rows, 1), 0, top)
    return jnp.take_along_axis(listing, (jnp.arange(top)[None, :] + rotation) % top, axis=1)


def shares(number_of, total, most, skew, full):
    portions = [(1 << 20) // math.isqrt(standing ** skew) + 1 for standing in range(1, number_of + 1)]
    largest = most if full else min(most, max(-(-total // number_of), total * portions[0] // sum(portions)))
    least = 1 if total - largest >= number_of - 1 else 0
    holding, rest = [largest] + [least] * (number_of - 1), total - largest - least * (number_of - 1)
    while rest > 0:
        movable = [i for i in range(1, number_of) if holding[i] < largest] or [i for i in range(1, number_of) if holding[i] < most]
        pool, remaining = sum([portions[i] for i in movable]), rest
        for i in movable:
            more = min(most - holding[i], max(1, remaining * portions[i] // pool), rest)
            holding[i] = holding[i] + more
            rest = rest - more
    return np.array(holding)


def normal_values(key, extent, spread, most, shards=(), held_as=jnp.bfloat16):
    array = jax.random.normal(key, extent, jnp.float32) * spread
    if len(shards) > 0:
        array = level_of(key, extent, shards, -0.22, 0.18) * array
    return jnp.clip(array, min=-most, max=most).astype(held_as)


def setup_inputs(seed: int = 0) -> dict:
    splits = jax.random.split(jax.random.key(seed), 7)
    tokens = normal_values(splits[0], (TOKENS, D), 1.0, 6.0, ((0, 32), (1, 8)))
    routes_keys = jax.random.split(jax.random.fold_in(splits[1], 1), TOKENS // TOK_DEV)
    routes_turns = jax.random.permutation(jax.random.fold_in(splits[1], 3), TOKENS // TOK_DEV)
    routes = jax.vmap(lambda own, number: routed_block(jax.random.fold_in(splits[1], 2), own, number, TOK_DEV, EXPERTS, TOP, CAP, 2))(routes_keys, routes_turns).reshape((TOKENS, TOP))
    gate_scales = jnp.clip(0.1 + 0.4 * jax.random.uniform(splits[2], (TOKENS, TOP), jnp.float32) ** level_of(splits[2], (TOKENS, TOP), ((0, 32),), -0.2, 0.2), 0.1, 0.5)
    gate_weight = normal_values(splits[3], (EXPERTS, D, FF), D ** -0.5, 0.0625, ((0, 32), (2, 8)))
    up_weight = normal_values(splits[4], (EXPERTS, D, FF), D ** -0.5, 0.0625, ((0, 32), (2, 8)))
    down_weight = normal_values(splits[5], (EXPERTS, FF, D), FF ** -0.5, 0.125, ((0, 32), (2, 8)))
    return {"tokens": tokens, "routes": routes, "gate_scales": gate_scales, "gate_weight": gate_weight, "up_weight": up_weight, "down_weight": down_weight}


def slot_targets(route_block):
    flat_ids = route_block.reshape(-1)
    onehot = (flat_ids[:, None] == jnp.arange(EXPERTS, dtype=jnp.int32)[None, :]).astype(jnp.int32)
    ranked = (jnp.cumsum(onehot, axis=0) - 1).astype(jnp.int32)
    slot_pos = jnp.sum(onehot * ranked, axis=1).astype(jnp.int32)
    return (flat_ids * CAP + slot_pos).astype(jnp.int32).reshape(route_block.shape)


def dispatch(target, token_rows):
    cell_ids = jnp.arange(EXPERTS * CAP, dtype=jnp.int32)
    tables = jnp.sum((target[None, :, :] == cell_ids[:, None, None]).astype(jnp.float32), axis=2).astype(jnp.bfloat16)
    return jnp.dot(tables, token_rows, preferred_element_type=jnp.float32).astype(jnp.bfloat16)


def expert_layer(pieces):
    inputs, w_gate, w_up, w_down = pieces
    gate_sum = jnp.dot(inputs, w_gate, preferred_element_type=jnp.float32)
    up_sum = jnp.dot(inputs, w_up, preferred_element_type=jnp.float32)
    hidden = (jax.nn.silu(gate_sum) * up_sum).astype(jnp.bfloat16)
    return jnp.dot(hidden, w_down, preferred_element_type=jnp.float32).astype(jnp.bfloat16)


def combine(pieces):
    returned_rows, target, scales = pieces
    picked = jnp.take(returned_rows, target.reshape(-1), axis=0)
    picked = picked.reshape(target.shape + (returned_rows.shape[1],)).astype(jnp.float32)
    return jnp.sum(scales[:, :, None] * picked, axis=1).astype(jnp.bfloat16)


def reference(tokens, routes, gate_scales, gate_weight, up_weight, down_weight):
    route_blocks = routes.reshape(EXPERTS, TOK_DEV, TOP)
    targets = jax.vmap(slot_targets)(route_blocks)
    token_blocks = tokens.reshape(EXPERTS, TOK_DEV, D)
    buffers = lax.map(lambda pair: dispatch(pair[0], pair[1]), (targets, token_blocks))
    buffers = buffers.reshape(EXPERTS, EXPERTS, CAP, D)
    by_expert = jnp.swapaxes(buffers, 0, 1).reshape(EXPERTS, EXPERTS * CAP, D)
    outputs = lax.map(expert_layer, (by_expert, gate_weight, up_weight, down_weight))
    outputs = outputs.reshape(EXPERTS, EXPERTS, CAP, D)
    by_source = jnp.swapaxes(outputs, 0, 1).reshape(EXPERTS, EXPERTS * CAP, D)
    scale_blocks = gate_scales.reshape(EXPERTS, TOK_DEV, TOP)
    mixed = lax.map(combine, (by_source, targets, scale_blocks))
    return mixed.reshape(TOKENS, D)
```

```python
import jax
import jax.numpy as jnp
from jax import lax
from jax.experimental import pallas as pl
from jax.experimental.pallas import tpu as pltpu
from jax.sharding import PartitionSpec as P

NX, NZ, NY, NC = 4, 8, 4, 2
CAP = 40
META = 128
AXES = ("expert", "tensor")
BF = jnp.bfloat16
F32 = jnp.float32


def pairs(move, keep=lambda x, z, y, c: True):
    out = []
    for x in range(NX):
        for z in range(NZ):
            for y in range(NY):
                for c in range(NC):
                    if keep(x, z, y, c):
                        a, b, d, e = move(x, z, y, c)
                        out.append((((x * NZ + z) * NY + y) * NC + c, ((a * NZ + b) * NY + d) * NC + e))
    return out


def first(c):
    return 1 if c == 0 else 3


def second(c):
    return 3 if c == 0 else 1


SWAP = pairs(lambda x, z, y, c: (x, z, y, 1 - c))
XP = pairs(lambda x, z, y, c: (x ^ first(c), z, y, c))
XQ = pairs(lambda x, z, y, c: (x ^ second(c), z, y, c))
YP = pairs(lambda x, z, y, c: (x, z, y ^ first(c), c))
YQ = pairs(lambda x, z, y, c: (x, z, y ^ second(c), c))
ZIN = pairs(lambda x, z, y, c: (x, (z + (2 * c - 1)) % NZ, y, c))
ZIN1 = pairs(lambda x, z, y, c: (x, (z + (2 * c - 1)) % NZ, y, c), lambda x, z, y, c: c == 1)
ZOUT = pairs(lambda x, z, y, c: (x, (z - (2 * c - 1)) % NZ, y, c))
ZOUT1 = pairs(lambda x, z, y, c: (x, (z - (2 * c - 1)) % NZ, y, c), lambda x, z, y, c: c == 1)


def send(value, perm):
    return lax.ppermute(value, AXES, perm)


def call(body, name, out_shape, grid=(), in_specs=None, out_specs=None, scratch=(), flops=0, moved=0, args=()):
    return pl.pallas_call(
        body,
        name=name,
        out_shape=out_shape,
        grid_spec=pltpu.PrefetchScalarGridSpec(
            num_scalar_prefetch=1,
            grid=grid,
            in_specs=in_specs,
            out_specs=out_specs,
            scratch_shapes=list(scratch),
        ),
        compiler_params=pltpu.CompilerParams(vmem_limit_bytes=24 * 1024 * 1024),
        cost_estimate=pl.CostEstimate(flops=flops, bytes_accessed=moved, transcendentals=0),
    )(*args)


def whole(shape):
    return pl.BlockSpec(shape, lambda *_: (0,) * len(shape))


def iota(shape, dim):
    return lax.broadcasted_iota(jnp.int32, shape, dim)


def prepare_body(sc, own, other, routes, scales, out):
    n = own.shape[0]
    lane = iota((n, META), 1)
    expert = lax.rem(lane, 32)
    group = lax.div(lane, 32)
    chosen = jnp.zeros((n, META), F32)
    scale = jnp.zeros((n, META), F32)
    for k in range(routes.shape[1]):
        hit = routes[:, k : k + 1] == expert
        chosen = chosen + jnp.where(hit, 1.0, 0.0)
        scale = scale + jnp.where(hit, scales[:, k : k + 1], 0.0)
    earlier = jnp.where(iota((n, n), 1) < iota((n, n), 0), 1.0, 0.0).astype(BF)
    slot = jnp.dot(earlier, chosen.astype(BF), preferred_element_type=F32)
    slot = jnp.where(chosen > 0.0, slot, -1.0)
    high = scale.astype(BF).astype(F32)
    low = scale - high
    meta = jnp.where(group == 0, slot, jnp.where(group == 1, high, jnp.where(group == 2, low, 0.0)))
    w = own.shape[1]
    out[:, :w] = own[...]
    out[:, w : 2 * w] = other[...]
    out[:, 2 * w :] = meta.astype(BF)


def prepare(sc, own, other, routes, scales):
    n, w = own.shape
    return call(
        prepare_body,
        "prepare",
        jax.ShapeDtypeStruct((n, 2 * w + META), BF),
        (1,),
        [whole(own.shape), whole(other.shape), whole(routes.shape), whole(scales.shape)],
        whole((n, 2 * w + META)),
        flops=2 * n * n * META,
        moved=8 * n * w,
        args=(sc, own, other, routes, scales),
    )


def row_pick(rows, experts, base):
    r = iota((rows, META), 0)
    col = iota((rows, META), 1)
    want = jnp.full((rows, META), -1, jnp.int32)
    for i, e in enumerate(experts):
        if e is not None:
            want = jnp.where((r >= i * CAP) & (r < (i + 1) * CAP), e + base, want)
    return jnp.where(col == want, 1.0, 0.0).astype(BF)


def nt(a, b):
    return lax.dot_general(a, b, (((1,), (1,)), ((), ())), preferred_element_type=F32)


def dispatch_body(sc, msg, keep, mid, far):
    w = keep.shape[1]
    n = msg.shape[0]
    meta = msg[:, w:]
    feats = msg[:, :w]
    for out, experts in ((keep, (sc[0],)), (mid, (sc[2],)), (far, (sc[1], sc[3]))):
        rows = out.shape[0]
        pos = nt(row_pick(rows, experts, 0), meta)
        slot = lax.rem(iota((rows, n), 0), CAP).astype(F32)
        table = jnp.where(pos == slot, 1.0, 0.0).astype(BF)
        out[...] = jnp.dot(table, feats, preferred_element_type=F32).astype(BF)


def dispatch(sc, msg):
    n, full = msg.shape
    w = full - META
    return call(
        dispatch_body,
        "dispatch",
        [jax.ShapeDtypeStruct((r * CAP, w), BF) for r in (1, 1, 2)],
        (1,),
        [whole(msg.shape)],
        [whole((r * CAP, w)) for r in (1, 1, 2)],
        flops=8 * CAP * n * w,
        moved=2 * (n * full + 4 * CAP * w),
        args=(sc, msg),
    )


def gate_up_body(sc, x0, x1, x2, x3, g_own, u_own, g_other, u_other, out, ga, ua, gb, ub):
    step = pl.program_id(0)
    k = g_own.shape[0]
    n = g_own.shape[1]
    for s in range(8):

        @pl.when(step == s)
        def _(s=s):
            x = (x0, x1, x2, x3)[s // 2][:, (s % 2) * k : (s % 2 + 1) * k]
            for acc, w in ((ga, g_own), (ua, u_own), (gb, g_other), (ub, u_other)):
                part = jnp.dot(x, w[...], preferred_element_type=F32)
                if s == 0:
                    acc[...] = part
                else:
                    acc[...] += part

    @pl.when(step == 7)
    def _():
        for i, (g, u) in enumerate(((ga, ua), (gb, ub))):
            v = g[...]
            out[:, i * n : (i + 1) * n] = (v / (1.0 + jnp.exp(-v)) * u[...]).astype(BF)


def gate_up(sc, pieces, weights):
    rows, w = pieces[0].shape
    k = w // 2
    n = weights[0].shape[1]
    block = pl.BlockSpec((k, n), lambda i, sc: (sc[4 + i], 0))
    return call(
        gate_up_body,
        "gate_up",
        jax.ShapeDtypeStruct((rows, 2 * n), BF),
        (8,),
        [whole((rows, w))] * 4 + [block] * 4,
        whole((rows, 2 * n)),
        [pltpu.VMEM((rows, n), F32)] * 4,
        flops=2 * rows * 8 * k * 4 * n,
        moved=2 * (4 * rows * w + 8 * k * 4 * n),
        args=(sc, *pieces, *weights),
    )


def down_body(sc, h0, h1, h2, h3, d_own, d_other, out, acc):
    step = pl.program_id(0)
    k, n = d_own.shape
    for s in range(8):

        @pl.when(step == s)
        def _(s=s):
            h = (h0, h1, h2, h3)[s // 2][:, (s % 2) * k : (s % 2 + 1) * k]
            for i, w in enumerate((d_own, d_other)):
                part = jnp.dot(h, w[...], preferred_element_type=F32)
                if s == 0:
                    acc[:, i * n : (i + 1) * n] = part
                elif s < 7:
                    acc[:, i * n : (i + 1) * n] += part
                else:
                    out[:, i * n : (i + 1) * n] = (acc[:, i * n : (i + 1) * n] + part).astype(BF)


def down(sc, pieces, weights):
    rows, w = pieces[0].shape
    k = w // 2
    n = weights[0].shape[1]
    block = pl.BlockSpec((k, n), lambda i, sc: (sc[4 + i], 0))
    return call(
        down_body,
        "down",
        jax.ShapeDtypeStruct((rows, 2 * n), BF),
        (8,),
        [whole((rows, w))] * 4 + [block] * 2,
        whole((rows, 2 * n)),
        [pltpu.VMEM((rows, 2 * n), F32)],
        flops=2 * rows * 8 * k * 2 * n,
        moved=2 * (4 * rows * w + 8 * k * 2 * n + rows * 2 * n),
        args=(sc, *pieces, *weights),
    )


def combine_body(sc, meta_ref, r0, r1, r2, *rest):
    acc, out = (rest[0], rest[1]) if len(rest) == 2 else (None, rest[0])
    meta = meta_ref[...]
    n = meta.shape[0]
    total = None if acc is None else acc[...].astype(F32)
    for ref, experts in ((r0, (sc[0], None, None, None)), (r1, (sc[2], None)), (r2, (sc[1], sc[3]))):
        rows = ref.shape[0]
        values = ref[...]
        pos = nt(meta, row_pick(rows, experts, 0))
        lane = iota((n, rows), 1)
        here = pos == lax.rem(lane, CAP).astype(F32)
        live = len([e for e in experts if e is not None]) * CAP
        if live < rows:
            here = here & (lane < live)
        for base in (32, 64):
            scale = nt(meta, row_pick(rows, experts, base))
            weight = jnp.where(here, scale, 0.0).astype(BF)
            part = jnp.dot(weight, values, preferred_element_type=F32)
            total = part if total is None else total + part
    out[...] = total.astype(out.dtype)


def combine(sc, meta, rows, acc, dtype):
    n = meta.shape[0]
    w = rows[0].shape[1]
    args = [meta, *rows] + ([] if acc is None else [acc])
    return call(
        combine_body,
        "combine",
        jax.ShapeDtypeStruct((n, w), dtype),
        (1,),
        [whole(a.shape) for a in args],
        whole((n, w)),
        flops=2 * n * w * 8 * CAP * 2,
        moved=2 * 8 * CAP * w + 8 * n * w,
        args=(sc, *args),
    )


def gather_y(value):
    one = send(value, YP)
    two = send(value, YQ)
    three = send(one, YQ)
    return value, one, two, three


def on_device(tokens, routes, gate_scales, gate_weight, up_weight, down_weight):
    w = tokens.shape[1]
    expert = lax.axis_index("expert")
    tensor = lax.axis_index("tensor")
    x, z = expert // NZ, expert % NZ
    y, c = tensor // NC, tensor % NC
    p, q = 1 + 2 * c, 3 - 2 * c
    rel = (0, p, q, 2)
    scalars = [(x ^ r) * NZ + z for r in rel]
    scalars += [(y ^ r) * NC + (c ^ h) for r in rel for h in (0, 1)]
    sc = jnp.stack([jnp.asarray(s, jnp.int32) for s in scalars])

    message = prepare(sc, tokens, send(tokens, SWAP), routes, gate_scales)
    wg, wu, wd = gate_weight[0], up_weight[0], down_weight[0]
    first_pair = (wg, wu, send(wg, SWAP), send(wu, SWAP))
    down_pair = (wd, send(wd, SWAP))

    held = [message]
    for k in range(4):
        held.append(send(held[-1], ZIN if k < 3 else ZIN1))
    blocks = {k: held[k] for k in (1, 2, 3)}
    blocks[4] = jnp.where(c == 0, held[0], held[4])

    def forward(block):
        keep, mid, far = dispatch(sc, block)
        got = send(far, XP)
        got2 = send(jnp.concatenate([mid, got[CAP:]], axis=0), XQ)
        rows = jnp.concatenate([keep, got[:CAP], got2], axis=0)
        hidden = gate_up(sc, gather_y(rows), first_pair)
        out = down(sc, gather_y(hidden), down_pair)
        back = send(out[2 * CAP :], XQ)
        back2 = send(jnp.concatenate([out[CAP : 2 * CAP], back[CAP:]], axis=0), XP)
        return out, back, back2

    results = {k: forward(blocks[k]) for k in (2, 3, 4, 1)}
    metas = {k: blocks[k][:, 2 * w :] for k in blocks}

    part4 = combine(sc, metas[4], results[4], None, F32)
    chain = send(part4, ZOUT1)
    for k in (3, 2, 1):
        chain = send(combine(sc, metas[k], results[k], chain, F32), ZOUT)
    home = chain + jnp.where(c == 0, part4, 0.0)
    return (home[:, :w] + send(home[:, w:], SWAP)).astype(BF)


def solution(mesh):
    in_specs = (
        P("expert", "tensor"),
        P("expert", None),
        P("expert", None),
        P("expert", None, "tensor"),
        P("expert", None, "tensor"),
        P("expert", None, "tensor"),
    )
    return jax.shard_map(
        on_device, mesh=mesh, in_specs=in_specs, out_specs=P("expert", "tensor"), check_vma=False
    )
```

```python
import jax
import jax.numpy as jnp
from jax import lax
from jax.experimental import pallas as pl
from jax.experimental.pallas import tpu as pltpu
from jax.sharding import PartitionSpec as P

NX, NZ, NY, NC = 4, 8, 4, 2
CAP = 40
META = 128
AXES = ("expert", "tensor")
BF = jnp.bfloat16
F32 = jnp.float32
ORDER = (1, 3, 4, 2)


def pairs(move, keep=lambda x, z, y, c: True):
    out = []
    for x in range(NX):
        for z in range(NZ):
            for y in range(NY):
                for c in range(NC):
                    if keep(x, z, y, c):
                        a, b, d, e = move(x, z, y, c)
                        out.append((((x * NZ + z) * NY + y) * NC + c, ((a * NZ + b) * NY + d) * NC + e))
    return out


def first(c):
    return 1 if c == 0 else 3


def second(c):
    return 3 if c == 0 else 1


SWAP = pairs(lambda x, z, y, c: (x, z, y, 1 - c))
XP = pairs(lambda x, z, y, c: (x ^ first(c), z, y, c))
XQ = pairs(lambda x, z, y, c: (x ^ second(c), z, y, c))
YP = pairs(lambda x, z, y, c: (x, z, y ^ first(c), c))
YQ = pairs(lambda x, z, y, c: (x, z, y ^ second(c), c))
X2 = pairs(lambda x, z, y, c: (x ^ 2, z, y, c))
Y2 = pairs(lambda x, z, y, c: (x, z, y ^ 2, c))
ZIN = pairs(lambda x, z, y, c: (x, (z + (2 * c - 1)) % NZ, y, c))
ZIN1 = pairs(lambda x, z, y, c: (x, (z + (2 * c - 1)) % NZ, y, c), lambda x, z, y, c: c == 1)
ZOUT = pairs(lambda x, z, y, c: (x, (z - (2 * c - 1)) % NZ, y, c))
ZOUT1 = pairs(lambda x, z, y, c: (x, (z - (2 * c - 1)) % NZ, y, c), lambda x, z, y, c: c == 1)


def send(value, perm):
    return lax.ppermute(value, AXES, perm)


def vmem(value):
    return pltpu.with_memory_space_constraint(value, pltpu.VMEM)


def call(body, name, out_shape, sc, *args, flops=0, after=()):
    moved = 2 * sum(a.size for a in args)
    spec = pl.BlockSpec(memory_space=pltpu.VMEM)
    count = 1 + len(args)

    def run(*refs):
        body(*refs[:count], *refs[count + len(after) :])

    return pl.pallas_call(
        run,
        name=name,
        out_shape=out_shape,
        in_specs=[pl.BlockSpec(memory_space=pltpu.SMEM)] + [spec] * len(args) + [pl.BlockSpec(memory_space=pl.ANY)] * len(after),
        out_specs=jax.tree.map(lambda _: spec, out_shape),
        compiler_params=pltpu.CompilerParams(vmem_limit_bytes=16 * 1024 * 1024),
        cost_estimate=pl.CostEstimate(flops=flops, bytes_accessed=moved, transcendentals=0),
    )(sc, *[vmem(a) for a in args], *after)


def iota(shape, dim):
    return lax.broadcasted_iota(jnp.int32, shape, dim)


def prepare_body(sc, own, other, routes, scales, out):
    n = own.shape[0]
    lane = iota((n, META), 1)
    expert = lax.rem(lane, 32)
    group = lax.div(lane, 32)
    chosen = jnp.zeros((n, META), F32)
    scale = jnp.zeros((n, META), F32)
    for k in range(routes.shape[1]):
        hit = routes[:, k : k + 1] == expert
        chosen = chosen + jnp.where(hit, 1.0, 0.0)
        scale = scale + jnp.where(hit, scales[:, k : k + 1], 0.0)
    earlier = jnp.where(iota((n, n), 1) < iota((n, n), 0), 1.0, 0.0).astype(BF)
    slot = jnp.dot(earlier, chosen.astype(BF), preferred_element_type=F32)
    slot = jnp.where(chosen > 0.0, slot, -1.0)
    high = scale.astype(BF).astype(F32)
    low = scale - high
    meta = jnp.where(group == 0, slot, jnp.where(group == 1, high, jnp.where(group == 2, low, 0.0)))
    w = own.shape[1]
    out[:, 2 * w :] = meta.astype(BF)
    for core in range(NC):

        @pl.when(sc[8] == core)
        def _(core=core):
            out[:, core * w : (core + 1) * w] = own[...]
            out[:, (1 - core) * w : (2 - core) * w] = other[...]


def prepare(sc, own, other, routes, scales):
    n, w = own.shape
    shape = jax.ShapeDtypeStruct((n, 2 * w + META), BF)
    return call(prepare_body, "prepare", shape, sc, own, other, routes, scales, flops=2 * n * n * META)


def row_pick(rows, experts, base):
    r = iota((rows, META), 0)
    col = iota((rows, META), 1)
    want = jnp.full((rows, META), -1, jnp.int32)
    for i, e in enumerate(experts):
        want = jnp.where((r >= i * CAP) & (r < (i + 1) * CAP), e + base, want)
    return jnp.where(col == want, 1.0, 0.0).astype(BF)


def nt(a, b):
    return lax.dot_general(a, b, (((1,), (1,)), ((), ())), preferred_element_type=F32)


def dispatch_body(sc, msg, *outs):
    w = outs[0].shape[1]
    n = msg.shape[0]
    rows = 4 * CAP
    pos = nt(row_pick(rows, [sc[j] for j in range(4)], 0), msg[:, w:])
    slot = lax.rem(iota((rows, n), 0), CAP).astype(F32)
    table = jnp.where(pos == slot, 1.0, 0.0).astype(BF)
    picked = jnp.dot(table, msg[:, :w], preferred_element_type=F32)
    for j in range(4):
        outs[j][...] = picked[j * CAP : (j + 1) * CAP].astype(BF)
    if len(outs) == 5:
        outs[4][...] = msg[...]


def dispatch(sc, msg, onward, after=()):
    n, full = msg.shape
    w = full - META
    shapes = [jax.ShapeDtypeStruct((CAP, w), BF)] * 4
    if onward:
        shapes = shapes + [jax.ShapeDtypeStruct(msg.shape, BF)]
    return call(dispatch_body, "dispatch", shapes, sc, msg, flops=8 * CAP * n * w, after=after)


def matmul(pieces, weight, sc):
    total = None
    for s in range(4):
        pair = pieces[s // 2]
        n, k = pair.shape[0] // 2, pair.shape[1]
        rows = pl.ds(pl.multiple_of(sc[4 + s] * k, 256), k)
        x = pair[s % 2 * n : (s % 2 + 1) * n, :]
        part = jnp.dot(x, weight[rows, :], preferred_element_type=F32)
        total = part if total is None else total + part
    return total


def gate_up_body(sc, near, far, g_own, u_own, g_other, u_other, out):
    n = g_own.shape[1]
    halves = []
    for gw, uw in ((g_own, u_own), (g_other, u_other)):
        v = matmul((near, far), gw, sc)
        u = matmul((near, far), uw, sc)
        halves.append((v / (1.0 + jnp.exp(-v)) * u).astype(BF))
    for core in range(NC):

        @pl.when(sc[8] == core)
        def _(core=core):
            out[:, core * n : (core + 1) * n] = halves[0]
            out[:, (1 - core) * n : (2 - core) * n] = halves[1]


def gate_up(sc, pieces, weights):
    rows, w = pieces[0].shape[0] // 2, pieces[0].shape[1]
    n = weights[0].shape[1]
    shape = jax.ShapeDtypeStruct((rows, 2 * n), BF)
    return call(gate_up_body, "gate_up", shape, sc, *pieces, *weights, flops=2 * rows * 4 * w * 4 * n)


def down_body(sc, near, far, d_own, d_other, *outs):
    n = d_own.shape[1]
    for i, w in enumerate((d_own, d_other)):
        total = matmul((near, far), w, sc)
        for j in range(4):
            outs[j][:, i * n : (i + 1) * n] = total[j * CAP : (j + 1) * CAP].astype(BF)


def down(sc, pieces, weights):
    rows, w = pieces[0].shape[0] // 2, pieces[0].shape[1]
    n = weights[0].shape[1]
    shapes = [jax.ShapeDtypeStruct((CAP, 2 * n), BF)] * 4
    return call(down_body, "down", shapes, sc, *pieces, *weights, flops=2 * rows * 4 * w * 2 * n)


def combine_body(sc, msg, rows_ref, *rest):
    out = rest[-1]
    w = out.shape[1]
    meta = msg[:, w:]
    n = meta.shape[0]
    rows = rows_ref.shape[0]
    experts = [sc[j] for j in range(4)]
    here = nt(meta, row_pick(rows, experts, 0)) == lax.rem(iota((n, rows), 1), CAP).astype(F32)
    weight = [jnp.where(here, nt(meta, row_pick(rows, experts, base)), 0.0) for base in (32, 64)]
    part = jnp.dot(jnp.concatenate(weight, axis=0).astype(BF), rows_ref[...], preferred_element_type=F32)
    total = part[:n] + part[n:]
    for ref in rest[:-1]:
        total = total + ref[...].astype(F32)
    out[...] = total.astype(out.dtype)


def combine(sc, msg, rows, acc, dtype):
    n = msg.shape[0]
    w = rows.shape[1]
    shape = jax.ShapeDtypeStruct((n, w), dtype)
    return call(combine_body, "combine", shape, sc, msg, rows, *acc, flops=4 * n * w * 4 * CAP)


def gather_y(value):
    pair = jnp.concatenate([value, send(value, YP)], axis=0)
    return pair, send(pair, YQ)


def exchange_x(own, p, q, two):
    return jnp.concatenate([own, send(p, XP), send(q, XQ), send(two, X2)], axis=0)


def on_device(tokens, routes, gate_scales, gate_weight, up_weight, down_weight):
    w = tokens.shape[1]
    expert = lax.axis_index("expert")
    tensor = lax.axis_index("tensor")
    x, z = expert // NZ, expert % NZ
    y, c = tensor // NC, tensor % NC
    rel = (0, 1 + 2 * c, 3 - 2 * c, 2)
    scalars = [(x ^ r) * NZ + z for r in rel] + [y ^ r for r in rel] + [c]
    sc = jnp.stack([jnp.asarray(s, jnp.int32) for s in scalars])

    wg, wu, wd = gate_weight[0], up_weight[0], down_weight[0]
    first_pair = (wg, wu, send(wg, SWAP), send(wu, SWAP))
    down_pair = (wd, send(wd, SWAP))
    early = {1: first_pair[2:], 2: down_pair[1:], 3: ()}

    held = [prepare(sc, tokens, send(tokens, SWAP), routes, gate_scales)]
    block, routed = {}, {}
    for k in (1, 2, 3):
        block[k] = send(held[-1], ZIN)
        *routed[k], onward = dispatch(sc, block[k], True, early[k])
        held.append(onward)
    block[4] = jnp.where(c == 0, held[0], send(held[-1], ZIN1))
    routed[4] = dispatch(sc, block[4], False)

    def experts(k):
        rows = exchange_x(*routed[k])
        hidden = gate_up(sc, gather_y(rows), first_pair)
        return exchange_x(*down(sc, gather_y(hidden), down_pair))

    rows = {k: experts(k) for k in ORDER}
    part4 = combine(sc, block[4], rows[4], (), F32)
    chain = send(part4, ZOUT1)
    for k in (3, 2, 1):
        kind = F32 if k == 3 else BF
        chain = send(combine(sc, block[k], rows[k], (chain,), kind), ZOUT)
    home = chain.astype(F32) + jnp.where(c == 0, part4, 0.0)
    return (home[:, :w] + send(home[:, w:], SWAP)).astype(BF)


def solution(mesh):
    in_specs = (
        P("expert", "tensor"),
        P("expert", None),
        P("expert", None),
        P("expert", None, "tensor"),
        P("expert", None, "tensor"),
        P("expert", None, "tensor"),
    )
    return jax.shard_map(
        on_device, mesh=mesh, in_specs=in_specs, out_specs=P("expert", "tensor"), check_vma=False
    )
```

```python
import jax
import jax.numpy as jnp
from jax import lax
from jax.experimental import pallas as pl
from jax.experimental.pallas import tpu as pltpu
from jax.sharding import PartitionSpec as P

NX, NZ, NY, NC = 4, 8, 4, 2
CAP = 40
META = 128
AXES = ("expert", "tensor")
BF = jnp.bfloat16
F32 = jnp.float32
ORDER = (1, 2, 3, 4)
LAG = 1


def pairs(move, keep=lambda x, z, y, c: True):
    out = []
    for x in range(NX):
        for z in range(NZ):
            for y in range(NY):
                for c in range(NC):
                    if keep(x, z, y, c):
                        a, b, d, e = move(x, z, y, c)
                        out.append((((x * NZ + z) * NY + y) * NC + c, ((a * NZ + b) * NY + d) * NC + e))
    return out


def first(c):
    return 1 if c == 0 else 3


def second(c):
    return 3 if c == 0 else 1


SWAP = pairs(lambda x, z, y, c: (x, z, y, 1 - c))
XP = pairs(lambda x, z, y, c: (x ^ first(c), z, y, c))
XQ = pairs(lambda x, z, y, c: (x ^ second(c), z, y, c))
YP = pairs(lambda x, z, y, c: (x, z, y ^ first(c), c))
YQ = pairs(lambda x, z, y, c: (x, z, y ^ second(c), c))
X2 = pairs(lambda x, z, y, c: (x ^ 2, z, y, c))
Y2 = pairs(lambda x, z, y, c: (x, z, y ^ 2, c))
ZIN = pairs(lambda x, z, y, c: (x, (z + (2 * c - 1)) % NZ, y, c))
ZIN1 = pairs(lambda x, z, y, c: (x, (z + (2 * c - 1)) % NZ, y, c), lambda x, z, y, c: c == 1)
ZOUT = {
    k: pairs(lambda x, z, y, c, k=k: (x, (z + k * (1 - 2 * c)) % NZ, y, c), lambda x, z, y, c, k=k: k < 4 or c == 1)
    for k in (1, 2, 3, 4)
}


def send(value, perm):
    return lax.ppermute(value, AXES, perm)


def vmem(value):
    return pltpu.with_memory_space_constraint(value, pltpu.VMEM)


def call(body, name, out_shape, sc, *args, flops=0, after=()):
    moved = 2 * sum(a.size for a in args)
    spec = pl.BlockSpec(memory_space=pltpu.VMEM)
    count = 1 + len(args)

    def run(*refs):
        body(*refs[:count], *refs[count + len(after) :])

    return pl.pallas_call(
        run,
        name=name,
        out_shape=out_shape,
        in_specs=[pl.BlockSpec(memory_space=pltpu.SMEM)] + [spec] * len(args) + [pl.BlockSpec(memory_space=pl.ANY)] * len(after),
        out_specs=jax.tree.map(lambda _: spec, out_shape),
        compiler_params=pltpu.CompilerParams(vmem_limit_bytes=16 * 1024 * 1024),
        cost_estimate=pl.CostEstimate(flops=flops, bytes_accessed=moved, transcendentals=0),
    )(sc, *[vmem(a) for a in args], *after)


def iota(shape, dim):
    return lax.broadcasted_iota(jnp.int32, shape, dim)


def prepare_body(sc, own, other, routes, scales, out):
    n = own.shape[0]
    lane = iota((n, META), 1)
    expert = lax.rem(lane, 32)
    group = lax.div(lane, 32)
    chosen = jnp.zeros((n, META), F32)
    scale = jnp.zeros((n, META), F32)
    for k in range(routes.shape[1]):
        hit = routes[:, k : k + 1] == expert
        chosen = chosen + jnp.where(hit, 1.0, 0.0)
        scale = scale + jnp.where(hit, scales[:, k : k + 1], 0.0)
    earlier = jnp.where(iota((n, n), 1) < iota((n, n), 0), 1.0, 0.0).astype(BF)
    slot = jnp.dot(earlier, chosen.astype(BF), preferred_element_type=F32)
    slot = jnp.where(chosen > 0.0, slot, -1.0)
    high = scale.astype(BF).astype(F32)
    low = scale - high
    meta = jnp.where(group == 0, slot, jnp.where(group == 1, high, jnp.where(group == 2, low, 0.0)))
    w = own.shape[1]
    out[:, 2 * w :] = meta.astype(BF)
    for core in range(NC):

        @pl.when(sc[8] == core)
        def _(core=core):
            out[:, core * w : (core + 1) * w] = own[...]
            out[:, (1 - core) * w : (2 - core) * w] = other[...]


def prepare(sc, own, other, routes, scales):
    n, w = own.shape
    shape = jax.ShapeDtypeStruct((n, 2 * w + META), BF)
    return call(prepare_body, "prepare", shape, sc, own, other, routes, scales, flops=2 * n * n * META)


def row_pick(rows, experts, base):
    r = iota((rows, META), 0)
    col = iota((rows, META), 1)
    want = jnp.full((rows, META), -1, jnp.int32)
    for i, e in enumerate(experts):
        want = jnp.where((r >= i * CAP) & (r < (i + 1) * CAP), e + base, want)
    return jnp.where(col == want, 1.0, 0.0).astype(BF)


def nt(a, b):
    return lax.dot_general(a, b, (((1,), (1,)), ((), ())), preferred_element_type=F32)


def dispatch_body(sc, msg, *outs):
    w = outs[0].shape[1]
    n = msg.shape[0]
    rows = 4 * CAP
    pos = nt(row_pick(rows, [sc[j] for j in range(4)], 0), msg[:, w:])
    slot = lax.rem(iota((rows, n), 0), CAP).astype(F32)
    table = jnp.where(pos == slot, 1.0, 0.0).astype(BF)
    picked = jnp.dot(table, msg[:, :w], preferred_element_type=F32)
    for j in range(4):
        outs[j][...] = picked[j * CAP : (j + 1) * CAP].astype(BF)
    if len(outs) == 5:
        outs[4][...] = msg[...]


def dispatch(sc, msg, onward, after=()):
    n, full = msg.shape
    w = full - META
    shapes = [jax.ShapeDtypeStruct((CAP, w), BF)] * 4
    if onward:
        shapes = shapes + [jax.ShapeDtypeStruct(msg.shape, BF)]
    return call(dispatch_body, "dispatch", shapes, sc, msg, flops=8 * CAP * n * w, after=after)


def matmul(pieces, weight, sc):
    total = None
    for s in range(4):
        pair = pieces[s // 2]
        n, k = pair.shape[0] // 2, pair.shape[1]
        rows = pl.ds(pl.multiple_of(sc[4 + s] * k, 256), k)
        x = pair[s % 2 * n : (s % 2 + 1) * n, :]
        part = jnp.dot(x, weight[rows, :], preferred_element_type=F32)
        total = part if total is None else total + part
    return total


def gate_up_body(sc, near, far, g_own, u_own, g_other, u_other, out):
    n = g_own.shape[1]
    halves = []
    for gw, uw in ((g_own, u_own), (g_other, u_other)):
        v = matmul((near, far), gw, sc)
        u = matmul((near, far), uw, sc)
        halves.append((v / (1.0 + jnp.exp(-v)) * u).astype(BF))
    for core in range(NC):

        @pl.when(sc[8] == core)
        def _(core=core):
            out[:, core * n : (core + 1) * n] = halves[0]
            out[:, (1 - core) * n : (2 - core) * n] = halves[1]


def gate_up(sc, pieces, weights, after=()):
    rows, w = pieces[0].shape[0] // 2, pieces[0].shape[1]
    n = weights[0].shape[1]
    shape = jax.ShapeDtypeStruct((rows, 2 * n), BF)
    return call(gate_up_body, "gate_up", shape, sc, *pieces, *weights, flops=2 * rows * 4 * w * 4 * n, after=after)


def down_body(sc, near, far, d_own, d_other, *outs):
    n = d_own.shape[1]
    for i, w in enumerate((d_own, d_other)):
        total = matmul((near, far), w, sc)
        for j in range(4):
            outs[j][:, i * n : (i + 1) * n] = total[j * CAP : (j + 1) * CAP].astype(BF)


def down(sc, pieces, weights, after=()):
    rows, w = pieces[0].shape[0] // 2, pieces[0].shape[1]
    n = weights[0].shape[1]
    shapes = [jax.ShapeDtypeStruct((CAP, 2 * n), BF)] * 4
    return call(down_body, "down", shapes, sc, *pieces, *weights, flops=2 * rows * 4 * w * 2 * n, after=after)


def combine_body(sc, msg, rows_ref, *rest):
    out = rest[-1]
    w = out.shape[1]
    meta = msg[:, w:]
    n = meta.shape[0]
    rows = rows_ref.shape[0]
    experts = [sc[j] for j in range(4)]
    here = nt(meta, row_pick(rows, experts, 0)) == lax.rem(iota((n, rows), 1), CAP).astype(F32)
    weight = [jnp.where(here, nt(meta, row_pick(rows, experts, base)), 0.0) for base in (32, 64)]
    part = jnp.dot(jnp.concatenate(weight, axis=0).astype(BF), rows_ref[...], preferred_element_type=F32)
    total = part[:n] + part[n:]
    for ref in rest[:-1]:
        total = total + ref[...].astype(F32)
    out[...] = total.astype(out.dtype)


def combine(sc, msg, rows, acc, dtype):
    n = msg.shape[0]
    w = rows.shape[1]
    shape = jax.ShapeDtypeStruct((n, w), dtype)
    return call(combine_body, "combine", shape, sc, msg, rows, *acc, flops=4 * n * w * 4 * CAP)


def gather_y(value):
    pair = jnp.concatenate([value, send(value, YP)], axis=0)
    return pair, send(pair, YQ)


def exchange_x(own, p, q, two):
    return jnp.concatenate([own, send(p, XP), send(q, XQ), send(two, X2)], axis=0)


def on_device(tokens, routes, gate_scales, gate_weight, up_weight, down_weight):
    w = tokens.shape[1]
    expert = lax.axis_index("expert")
    tensor = lax.axis_index("tensor")
    x, z = expert // NZ, expert % NZ
    y, c = tensor // NC, tensor % NC
    rel = (0, 1 + 2 * c, 3 - 2 * c, 2)
    scalars = [(x ^ r) * NZ + z for r in rel] + [y ^ r for r in rel] + [c]
    sc = jnp.stack([jnp.asarray(s, jnp.int32) for s in scalars])

    wg, wu, wd = gate_weight[0], up_weight[0], down_weight[0]
    first_pair = (wg, wu, send(wg, SWAP), send(wu, SWAP))
    down_pair = (wd, send(wd, SWAP))

    message = prepare(sc, tokens, send(tokens, SWAP), routes, gate_scales)
    block = {1: send(message, ZIN)}
    rows, wide, hidden, out, home = {}, {}, {}, {}, {}
    *routed, onward = dispatch(sc, block[1], True, first_pair[2:])
    block[2] = send(onward, ZIN)
    block[3] = send(block[2], ZIN)
    block[4] = jnp.where(c == 0, message, send(block[3], ZIN1))
    for i, k in enumerate(ORDER):
        if i > 0:
            before = ORDER[i - 1]
            routed = dispatch(sc, block[k], False, (rows[before],) if i > 1 else (wide[before][0], down_pair[1]))
        rows[k] = exchange_x(*routed)
        wide[k] = gather_y(rows[k])
    for i, k in enumerate(ORDER):
        after = () if i == 0 else (hidden[ORDER[i - 1]],)
        if i > LAG:
            after += (out[ORDER[i - 1 - LAG]][0],)
        hidden[k] = gate_up(sc, wide[k], first_pair, after)
        after = (home[ORDER[i - 2]],) if i > 1 else ()
        out[k] = down(sc, gather_y(hidden[k]), down_pair, after)
        home[k] = combine(sc, block[k], exchange_x(*out[k]), (), BF)
    total = jnp.where(c == 0, home[4], send(home[4], ZOUT[4])).astype(F32)
    for k in (1, 2, 3):
        total = total + send(home[k], ZOUT[k]).astype(F32)
    return (total[:, :w] + send(total[:, w:], SWAP)).astype(BF)


def solution(mesh):
    in_specs = (
        P("expert", "tensor"),
        P("expert", None),
        P("expert", None),
        P("expert", None, "tensor"),
        P("expert", None, "tensor"),
        P("expert", None, "tensor"),
    )
    return jax.shard_map(
        on_device, mesh=mesh, in_specs=in_specs, out_specs=P("expert", "tensor"), check_vma=False
    )
```

```python
import jax
import jax.numpy as jnp
from jax import lax
from jax.experimental import pallas as pl
from jax.experimental.pallas import tpu as pltpu
from jax.sharding import PartitionSpec as P

NX, NZ, NY, NC = 4, 8, 4, 2
CAP = 40
META = 128
AXES = ("expert", "tensor")
BF = jnp.bfloat16
F32 = jnp.float32
ORDER = (1, 2, 3, 4)
LAG = 1
HLAG = 2
CHAIN = True
SCALE = 1.0
XIN = True
XOUT = True
GATHER_X = 2
GATHER_H = 2
DEP = ('', 'n', 'r', 'r')
ONWARD = True
WEARLY = 0
END = 0


def pairs(move, keep=lambda x, z, y, c: True):
    out = []
    for x in range(NX):
        for z in range(NZ):
            for y in range(NY):
                for c in range(NC):
                    if keep(x, z, y, c):
                        a, b, d, e = move(x, z, y, c)
                        out.append((((x * NZ + z) * NY + y) * NC + c, ((a * NZ + b) * NY + d) * NC + e))
    return out


def first(c):
    return 1 if c == 0 else 3


def second(c):
    return 3 if c == 0 else 1


SWAP = pairs(lambda x, z, y, c: (x, z, y, 1 - c))
XP = pairs(lambda x, z, y, c: (x ^ first(c), z, y, c))
XQ = pairs(lambda x, z, y, c: (x ^ second(c), z, y, c))
YP = pairs(lambda x, z, y, c: (x, z, y ^ first(c), c))
YQ = pairs(lambda x, z, y, c: (x, z, y ^ second(c), c))
X2 = pairs(lambda x, z, y, c: (x ^ 2, z, y, c))
Y2 = pairs(lambda x, z, y, c: (x, z, y ^ 2, c))
ZIN = pairs(lambda x, z, y, c: (x, (z + (2 * c - 1)) % NZ, y, c))
ZIN1 = pairs(lambda x, z, y, c: (x, (z + (2 * c - 1)) % NZ, y, c), lambda x, z, y, c: c == 1)
ZOUT1 = pairs(lambda x, z, y, c: (x, (z - (2 * c - 1)) % NZ, y, c), lambda x, z, y, c: c == 1)
ZOUT = {
    k: pairs(lambda x, z, y, c, k=k: (x, (z + k * (1 - 2 * c)) % NZ, y, c), lambda x, z, y, c, k=k: k < 4 or c == 1)
    for k in (1, 2, 3, 4)
}


def send(value, perm):
    return lax.ppermute(value, AXES, perm)


def vmem(value):
    return pltpu.with_memory_space_constraint(value, pltpu.VMEM)


def call(body, name, out_shape, sc, *args, flops=0, after=()):
    moved = 2 * sum(a.size for a in args)
    spec = pl.BlockSpec(memory_space=pltpu.VMEM)
    count = 1 + len(args)

    def run(*refs):
        body(*refs[:count], *refs[count + len(after) :])

    return pl.pallas_call(
        run,
        name=name,
        out_shape=out_shape,
        in_specs=[pl.BlockSpec(memory_space=pltpu.SMEM)] + [spec] * len(args) + [pl.BlockSpec(memory_space=pl.ANY)] * len(after),
        out_specs=jax.tree.map(lambda _: spec, out_shape),
        compiler_params=pltpu.CompilerParams(vmem_limit_bytes=16 * 1024 * 1024),
        cost_estimate=pl.CostEstimate(flops=int(flops * SCALE), bytes_accessed=int(moved * SCALE), transcendentals=0),
    )(sc, *[vmem(a) for a in args], *after)


def iota(shape, dim):
    return lax.broadcasted_iota(jnp.int32, shape, dim)


def prepare_body(sc, own, other, routes, scales, out):
    n = own.shape[0]
    lane = iota((n, META), 1)
    expert = lax.rem(lane, 32)
    group = lax.div(lane, 32)
    chosen = jnp.zeros((n, META), F32)
    scale = jnp.zeros((n, META), F32)
    for k in range(routes.shape[1]):
        hit = routes[:, k : k + 1] == expert
        chosen = chosen + jnp.where(hit, 1.0, 0.0)
        scale = scale + jnp.where(hit, scales[:, k : k + 1], 0.0)
    earlier = jnp.where(iota((n, n), 1) < iota((n, n), 0), 1.0, 0.0).astype(BF)
    slot = jnp.dot(earlier, chosen.astype(BF), preferred_element_type=F32)
    slot = jnp.where(chosen > 0.0, slot, -1.0)
    high = scale.astype(BF).astype(F32)
    low = scale - high
    meta = jnp.where(group == 0, slot, jnp.where(group == 1, high, jnp.where(group == 2, low, 0.0)))
    w = own.shape[1]
    out[:, 2 * w :] = meta.astype(BF)
    for core in range(NC):

        @pl.when(sc[8] == core)
        def _(core=core):
            out[:, core * w : (core + 1) * w] = own[...]
            out[:, (1 - core) * w : (2 - core) * w] = other[...]


def prepare(sc, own, other, routes, scales):
    n, w = own.shape
    shape = jax.ShapeDtypeStruct((n, 2 * w + META), BF)
    return call(prepare_body, "prepare", shape, sc, own, other, routes, scales, flops=2 * n * n * META)


def row_pick(rows, experts, base):
    r = iota((rows, META), 0)
    col = iota((rows, META), 1)
    want = jnp.full((rows, META), -1, jnp.int32)
    for i, e in enumerate(experts):
        want = jnp.where((r >= i * CAP) & (r < (i + 1) * CAP), e + base, want)
    return jnp.where(col == want, 1.0, 0.0).astype(BF)


def nt(a, b):
    return lax.dot_general(a, b, (((1,), (1,)), ((), ())), preferred_element_type=F32)


def dispatch_body(sc, msg, *outs):
    w = outs[0].shape[1]
    n = msg.shape[0]
    rows = 4 * CAP
    pos = nt(row_pick(rows, [sc[j] for j in range(4)], 0), msg[:, w:])
    slot = lax.rem(iota((rows, n), 0), CAP).astype(F32)
    table = jnp.where(pos == slot, 1.0, 0.0).astype(BF)
    picked = jnp.dot(table, msg[:, :w], preferred_element_type=F32)
    for j in range(4):
        outs[j][...] = picked[j * CAP : (j + 1) * CAP].astype(BF)
    if len(outs) == 5:
        outs[4][...] = msg[...]


def dispatch(sc, msg, onward, after=()):
    n, full = msg.shape
    w = full - META
    shapes = [jax.ShapeDtypeStruct((CAP, w), BF)] * 4
    if onward:
        shapes = shapes + [jax.ShapeDtypeStruct(msg.shape, BF)]
    return call(dispatch_body, "dispatch", shapes, sc, msg, flops=8 * CAP * n * w, after=after)


def matmul(pieces, weight, sc):
    total = None
    for s in range(4):
        pair = pieces[s // 2]
        n, k = pair.shape[0] // 2, pair.shape[1]
        rows = pl.ds(pl.multiple_of(sc[4 + s] * k, 256), k)
        x = pair[s % 2 * n : (s % 2 + 1) * n, :]
        part = jnp.dot(x, weight[rows, :], preferred_element_type=F32)
        total = part if total is None else total + part
    return total


def gate_up_body(sc, near, far, g_own, u_own, g_other, u_other, out):
    n = g_own.shape[1]
    halves = []
    for gw, uw in ((g_own, u_own), (g_other, u_other)):
        v = matmul((near, far), gw, sc)
        u = matmul((near, far), uw, sc)
        halves.append((v / (1.0 + jnp.exp(-v)) * u).astype(BF))
    for core in range(NC):

        @pl.when(sc[8] == core)
        def _(core=core):
            out[:, core * n : (core + 1) * n] = halves[0]
            out[:, (1 - core) * n : (2 - core) * n] = halves[1]


def gate_up(sc, pieces, weights, after=()):
    rows, w = pieces[0].shape[0] // 2, pieces[0].shape[1]
    n = weights[0].shape[1]
    shape = jax.ShapeDtypeStruct((rows, 2 * n), BF)
    return call(gate_up_body, "gate_up", shape, sc, *pieces, *weights, flops=2 * rows * 4 * w * 4 * n, after=after)


def down_body(sc, near, far, d_own, d_other, *outs):
    n = d_own.shape[1]
    for i, w in enumerate((d_own, d_other)):
        total = matmul((near, far), w, sc)
        for j in range(4):
            outs[j][:, i * n : (i + 1) * n] = total[j * CAP : (j + 1) * CAP].astype(BF)


def down(sc, pieces, weights, after=()):
    rows, w = pieces[0].shape[0] // 2, pieces[0].shape[1]
    n = weights[0].shape[1]
    shapes = [jax.ShapeDtypeStruct((CAP, 2 * n), BF)] * 4
    return call(down_body, "down", shapes, sc, *pieces, *weights, flops=2 * rows * 4 * w * 2 * n, after=after)


def combine_body(sc, msg, rows_ref, *rest):
    out = rest[-1]
    w = out.shape[1]
    meta = msg[:, w:]
    n = meta.shape[0]
    rows = rows_ref.shape[0]
    experts = [sc[j] for j in range(4)]
    here = nt(meta, row_pick(rows, experts, 0)) == lax.rem(iota((n, rows), 1), CAP).astype(F32)
    weight = [jnp.where(here, nt(meta, row_pick(rows, experts, base)), 0.0) for base in (32, 64)]
    part = jnp.dot(jnp.concatenate(weight, axis=0).astype(BF), rows_ref[...], preferred_element_type=F32)
    total = part[:n] + part[n:]
    for ref in rest[:-1]:
        total = total + ref[...].astype(F32)
    out[...] = total.astype(out.dtype)


def combine(sc, msg, rows, acc, dtype):
    n = msg.shape[0]
    w = rows.shape[1]
    shape = jax.ShapeDtypeStruct((n, w), dtype)
    return call(combine_body, "combine", shape, sc, msg, rows, *acc, flops=4 * n * w * 4 * CAP)


def gather_y(value):
    pair = jnp.concatenate([value, send(value, YP)], axis=0)
    return pair, send(pair, YQ)


def exchange_x(own, p, q, two, direct):
    if direct:
        return jnp.concatenate([own, send(p, XP), send(q, XQ), send(two, X2)], axis=0)
    got = send(jnp.concatenate([p, two], axis=0), XP)
    got2 = send(jnp.concatenate([q, got[CAP:]], axis=0), XQ)
    return jnp.concatenate([own, got[:CAP], got2], axis=0)


def gather_three(value):
    one = send(value, YP)
    two = send(value, YQ)
    return jnp.concatenate([value, one], axis=0), jnp.concatenate([two, send(one, YQ)], axis=0)


def gather_direct(value):
    one = send(value, YP)
    two = send(value, YQ)
    return jnp.concatenate([value, one], axis=0), jnp.concatenate([two, send(value, Y2)], axis=0)


GY = {2: gather_y, 3: gather_three, 1: gather_direct}


def on_device(tokens, routes, gate_scales, gate_weight, up_weight, down_weight):
    w = tokens.shape[1]
    expert = lax.axis_index("expert")
    tensor = lax.axis_index("tensor")
    x, z = expert // NZ, expert % NZ
    y, c = tensor // NC, tensor % NC
    rel = (0, 1 + 2 * c, 3 - 2 * c, 2)
    scalars = [(x ^ r) * NZ + z for r in rel] + [y ^ r for r in rel] + [c]
    sc = jnp.stack([jnp.asarray(s, jnp.int32) for s in scalars])

    wg, wu, wd = gate_weight[0], up_weight[0], down_weight[0]
    swapped = send(tokens, SWAP)
    swapped, wg, wu = lax.optimization_barrier((swapped, wg, wu))
    message = prepare(sc, tokens, swapped, routes, gate_scales)
    first_pair = (wg, wu, send(wg, SWAP), send(wu, SWAP))
    message, wd = lax.optimization_barrier((message, wd))
    down_pair = (wd, send(wd, SWAP))

    block = {1: send(message, ZIN)}
    rows, wide, hidden, out, home = {}, {}, {}, {}, {}
    gx = GY[GATHER_X]
    gh = GY[GATHER_H]
    lead = ORDER[0]
    early = first_pair[2:] if WEARLY == 0 else ()
    if lead == 2:
        block[2] = send(block[1], ZIN)
    got = dispatch(sc, block[lead], ONWARD, early)
    routed = got[:4]
    onward = got[4] if ONWARD else block[lead]
    for k in range(lead + 1, 4):
        block[k] = send(onward, ZIN)
        onward = block[k]
    block[4] = jnp.where(c == 0, message, send(block[3], ZIN1))
    for i, k in enumerate(ORDER):
        if i > 0:
            before = ORDER[i - 1]
            after = ()
            kind = DEP[i]
            if 'r' in kind:
                after += (rows[before],)
            if 'n' in kind:
                after += (wide[before][0],)
            if 'f' in kind and i > 1:
                after += (wide[ORDER[i - 2]][1],)
            if 'h' in kind and i > 1:
                after += (hidden[ORDER[i - 2]],)
            if i == 1 + WEARLY and WEARLY:
                after += first_pair[2:]
            if i == 1:
                after += down_pair[1:]
            routed = dispatch(sc, block[k], False, after)
        rows[k] = exchange_x(*routed, XIN)
        wide[k] = gx(rows[k])
        after = ()
        if i > 0 and CHAIN:
            after += (hidden[ORDER[i - 1]],)
        if i > LAG:
            after += (out[ORDER[i - 1 - LAG]][0],)
        hidden[k] = gate_up(sc, wide[k], first_pair, after)
        after = (home[ORDER[i - HLAG]],) if i >= HLAG else ()
        out[k] = down(sc, gh(hidden[k]), down_pair, after)
        home[k] = combine(sc, block[k], exchange_x(*out[k], XOUT), (), BF if k == ORDER[3] or END == 0 else F32)
    f4 = home[4].astype(F32)
    if END == 0:
        total = jnp.where(c == 0, home[4], send(home[4], ZOUT[4])).astype(F32)
        for k in (1, 2, 3):
            total = total + send(home[k], ZOUT[k]).astype(F32)
    elif END == 1:
        chain = home[2].astype(F32) + send(home[3].astype(BF), ZOUT[1]).astype(F32)
        chain = home[1].astype(F32) + send(chain.astype(BF), ZOUT[1]).astype(F32)
        total = jnp.where(c == 0, home[4], send(home[4].astype(BF), ZOUT[4]).astype(home[4].dtype)).astype(F32)
        total = total + send(chain.astype(BF), ZOUT[1]).astype(F32)
    elif END == 2:
        chain = home[3].astype(F32) + send(home[4], ZOUT1).astype(F32)
        chain = home[1].astype(F32) + send(chain.astype(BF), ZOUT[2]).astype(F32)
        total = send(chain.astype(BF), ZOUT[1]).astype(F32) + send(home[2].astype(BF), ZOUT[2]).astype(F32)
        total = total + jnp.where(c == 0, f4, 0.0)
    else:
        chain = home[3].astype(F32) + send(home[4], ZOUT1).astype(F32)
        chain = home[2].astype(F32) + send(chain.astype(BF), ZOUT[1]).astype(F32)
        total = send(chain.astype(BF), ZOUT[2]).astype(F32) + send(home[1].astype(BF), ZOUT[1]).astype(F32)
        total = total + jnp.where(c == 0, f4, 0.0)
    return (total[:, :w] + send(total[:, w:], SWAP)).astype(BF)


def solution(mesh):
    in_specs = (
        P("expert", "tensor"),
        P("expert", None),
        P("expert", None),
        P("expert", None, "tensor"),
        P("expert", None, "tensor"),
        P("expert", None, "tensor"),
    )
    return jax.shard_map(
        on_device, mesh=mesh, in_specs=in_specs, out_specs=P("expert", "tensor"), check_vma=False
    )
```

```python
import jax
import jax.numpy as jnp
from jax import lax
from jax.experimental import pallas as pl
from jax.experimental.pallas import tpu as pltpu
from jax.sharding import PartitionSpec as P

NX, NZ, NY, NC = 4, 8, 4, 2
CAP = 40
META = 128
AXES = ("expert", "tensor")
BF = jnp.bfloat16
F32 = jnp.float32
ORDER = (1, 2, 3, 4)
LAG = 1
HLAG = 2
CHAIN = True
SCALE = 1.0
XIN = True
XOUT = True
GATHER_X = 2
GATHER_H = 2
DEP = ('', 'r', 'r', 'r')
ONWARD = True
WEARLY = 0
END = 0


def pairs(move, keep=lambda x, z, y, c: True):
    out = []
    for x in range(NX):
        for z in range(NZ):
            for y in range(NY):
                for c in range(NC):
                    if keep(x, z, y, c):
                        a, b, d, e = move(x, z, y, c)
                        out.append((((x * NZ + z) * NY + y) * NC + c, ((a * NZ + b) * NY + d) * NC + e))
    return out


def first(c):
    return 1 if c == 0 else 3


def second(c):
    return 3 if c == 0 else 1


SWAP = pairs(lambda x, z, y, c: (x, z, y, 1 - c))
XP = pairs(lambda x, z, y, c: (x ^ first(c), z, y, c))
XQ = pairs(lambda x, z, y, c: (x ^ second(c), z, y, c))
YP = pairs(lambda x, z, y, c: (x, z, y ^ first(c), c))
YQ = pairs(lambda x, z, y, c: (x, z, y ^ second(c), c))
X2 = pairs(lambda x, z, y, c: (x ^ 2, z, y, c))
Y2 = pairs(lambda x, z, y, c: (x, z, y ^ 2, c))
ZIN = pairs(lambda x, z, y, c: (x, (z + (2 * c - 1)) % NZ, y, c))
ZIN1 = pairs(lambda x, z, y, c: (x, (z + (2 * c - 1)) % NZ, y, c), lambda x, z, y, c: c == 1)
ZOUT1 = pairs(lambda x, z, y, c: (x, (z - (2 * c - 1)) % NZ, y, c), lambda x, z, y, c: c == 1)
ZOUT = {
    k: pairs(lambda x, z, y, c, k=k: (x, (z + k * (1 - 2 * c)) % NZ, y, c), lambda x, z, y, c, k=k: k < 4 or c == 1)
    for k in (1, 2, 3, 4)
}


def send(value, perm):
    return lax.ppermute(value, AXES, perm)


def vmem(value):
    return pltpu.with_memory_space_constraint(value, pltpu.VMEM)


def call(body, name, out_shape, sc, *args, flops=0, after=()):
    moved = 2 * sum(a.size for a in args)
    spec = pl.BlockSpec(memory_space=pltpu.VMEM)
    count = 1 + len(args)

    def run(*refs):
        body(*refs[:count], *refs[count + len(after) :])

    return pl.pallas_call(
        run,
        name=name,
        out_shape=out_shape,
        in_specs=[pl.BlockSpec(memory_space=pltpu.SMEM)] + [spec] * len(args) + [pl.BlockSpec(memory_space=pl.ANY)] * len(after),
        out_specs=jax.tree.map(lambda _: spec, out_shape),
        compiler_params=pltpu.CompilerParams(vmem_limit_bytes=16 * 1024 * 1024),
        cost_estimate=pl.CostEstimate(flops=int(flops * SCALE), bytes_accessed=int(moved * SCALE), transcendentals=0),
    )(sc, *[vmem(a) for a in args], *after)


def iota(shape, dim):
    return lax.broadcasted_iota(jnp.int32, shape, dim)


def prepare_body(sc, own, other, routes, scales, out):
    n = own.shape[0]
    lane = iota((n, META), 1)
    expert = lax.rem(lane, 32)
    group = lax.div(lane, 32)
    chosen = jnp.zeros((n, META), F32)
    scale = jnp.zeros((n, META), F32)
    for k in range(routes.shape[1]):
        hit = routes[:, k : k + 1] == expert
        chosen = chosen + jnp.where(hit, 1.0, 0.0)
        scale = scale + jnp.where(hit, scales[:, k : k + 1], 0.0)
    earlier = jnp.where(iota((n, n), 1) < iota((n, n), 0), 1.0, 0.0).astype(BF)
    slot = jnp.dot(earlier, chosen.astype(BF), preferred_element_type=F32)
    slot = jnp.where(chosen > 0.0, slot, -1.0)
    high = scale.astype(BF).astype(F32)
    low = scale - high
    meta = jnp.where(group == 0, slot, jnp.where(group == 1, high, jnp.where(group == 2, low, 0.0)))
    w = own.shape[1]
    out[:, 2 * w :] = meta.astype(BF)
    for core in range(NC):

        @pl.when(sc[8] == core)
        def _(core=core):
            out[:, core * w : (core + 1) * w] = own[...]
            out[:, (1 - core) * w : (2 - core) * w] = other[...]


def prepare(sc, own, other, routes, scales):
    n, w = own.shape
    shape = jax.ShapeDtypeStruct((n, 2 * w + META), BF)
    return call(prepare_body, "prepare", shape, sc, own, other, routes, scales, flops=2 * n * n * META)


def row_pick(rows, experts, base):
    r = iota((rows, META), 0)
    col = iota((rows, META), 1)
    want = jnp.full((rows, META), -1, jnp.int32)
    for i, e in enumerate(experts):
        want = jnp.where((r >= i * CAP) & (r < (i + 1) * CAP), e + base, want)
    return jnp.where(col == want, 1.0, 0.0).astype(BF)


def nt(a, b):
    return lax.dot_general(a, b, (((1,), (1,)), ((), ())), preferred_element_type=F32)


def dispatch_body(sc, msg, *outs):
    w = outs[0].shape[1]
    n = msg.shape[0]
    rows = 4 * CAP
    pos = nt(row_pick(rows, [sc[j] for j in range(4)], 0), msg[:, w:])
    slot = lax.rem(iota((rows, n), 0), CAP).astype(F32)
    table = jnp.where(pos == slot, 1.0, 0.0).astype(BF)
    picked = jnp.dot(table, msg[:, :w], preferred_element_type=F32)
    for j in range(4):
        outs[j][...] = picked[j * CAP : (j + 1) * CAP].astype(BF)
    if len(outs) == 5:
        outs[4][...] = msg[...]


def dispatch(sc, msg, onward, after=()):
    n, full = msg.shape
    w = full - META
    shapes = [jax.ShapeDtypeStruct((CAP, w), BF)] * 4
    if onward:
        shapes = shapes + [jax.ShapeDtypeStruct(msg.shape, BF)]
    return call(dispatch_body, "dispatch", shapes, sc, msg, flops=8 * CAP * n * w, after=after)


def matmul(pieces, weight, sc):
    total = None
    for s in range(4):
        pair = pieces[s // 2]
        n, k = pair.shape[0] // 2, pair.shape[1]
        rows = pl.ds(pl.multiple_of(sc[4 + s] * k, 256), k)
        x = pair[s % 2 * n : (s % 2 + 1) * n, :]
        part = jnp.dot(x, weight[rows, :], preferred_element_type=F32)
        total = part if total is None else total + part
    return total


def gate_up_body(sc, near, far, g_own, u_own, g_other, u_other, out):
    n = g_own.shape[1]
    halves = []
    for gw, uw in ((g_own, u_own), (g_other, u_other)):
        v = matmul((near, far), gw, sc)
        u = matmul((near, far), uw, sc)
        halves.append((v / (1.0 + jnp.exp(-v)) * u).astype(BF))
    for core in range(NC):

        @pl.when(sc[8] == core)
        def _(core=core):
            out[:, core * n : (core + 1) * n] = halves[0]
            out[:, (1 - core) * n : (2 - core) * n] = halves[1]


def gate_up(sc, pieces, weights, after=()):
    rows, w = pieces[0].shape[0] // 2, pieces[0].shape[1]
    n = weights[0].shape[1]
    shape = jax.ShapeDtypeStruct((rows, 2 * n), BF)
    return call(gate_up_body, "gate_up", shape, sc, *pieces, *weights, flops=2 * rows * 4 * w * 4 * n, after=after)


def down_body(sc, near, far, d_own, d_other, *outs):
    n = d_own.shape[1]
    for i, w in enumerate((d_own, d_other)):
        total = matmul((near, far), w, sc)
        for j in range(4):
            outs[j][:, i * n : (i + 1) * n] = total[j * CAP : (j + 1) * CAP].astype(BF)


def down(sc, pieces, weights, after=()):
    rows, w = pieces[0].shape[0] // 2, pieces[0].shape[1]
    n = weights[0].shape[1]
    shapes = [jax.ShapeDtypeStruct((CAP, 2 * n), BF)] * 4
    return call(down_body, "down", shapes, sc, *pieces, *weights, flops=2 * rows * 4 * w * 2 * n, after=after)


def combine_body(sc, msg, rows_ref, *rest):
    out = rest[-1]
    w = out.shape[1]
    meta = msg[:, w:]
    n = meta.shape[0]
    rows = rows_ref.shape[0]
    experts = [sc[j] for j in range(4)]
    here = nt(meta, row_pick(rows, experts, 0)) == lax.rem(iota((n, rows), 1), CAP).astype(F32)
    weight = [jnp.where(here, nt(meta, row_pick(rows, experts, base)), 0.0) for base in (32, 64)]
    part = jnp.dot(jnp.concatenate(weight, axis=0).astype(BF), rows_ref[...], preferred_element_type=F32)
    total = part[:n] + part[n:]
    for ref in rest[:-1]:
        total = total + ref[...].astype(F32)
    out[...] = total.astype(out.dtype)


def combine(sc, msg, rows, acc, dtype):
    n = msg.shape[0]
    w = rows.shape[1]
    shape = jax.ShapeDtypeStruct((n, w), dtype)
    return call(combine_body, "combine", shape, sc, msg, rows, *acc, flops=4 * n * w * 4 * CAP)


def gather_y(value):
    pair = jnp.concatenate([value, send(value, YP)], axis=0)
    return pair, send(pair, YQ)


def exchange_x(own, p, q, two, direct):
    if direct:
        return jnp.concatenate([own, send(p, XP), send(q, XQ), send(two, X2)], axis=0)
    got = send(jnp.concatenate([p, two], axis=0), XP)
    got2 = send(jnp.concatenate([q, got[CAP:]], axis=0), XQ)
    return jnp.concatenate([own, got[:CAP], got2], axis=0)


def gather_three(value):
    one = send(value, YP)
    two = send(value, YQ)
    return jnp.concatenate([value, one], axis=0), jnp.concatenate([two, send(one, YQ)], axis=0)


def gather_direct(value):
    one = send(value, YP)
    two = send(value, YQ)
    return jnp.concatenate([value, one], axis=0), jnp.concatenate([two, send(value, Y2)], axis=0)


GY = {2: gather_y, 3: gather_three, 1: gather_direct}


def on_device(tokens, routes, gate_scales, gate_weight, up_weight, down_weight):
    w = tokens.shape[1]
    expert = lax.axis_index("expert")
    tensor = lax.axis_index("tensor")
    x, z = expert // NZ, expert % NZ
    y, c = tensor // NC, tensor % NC
    rel = (0, 1 + 2 * c, 3 - 2 * c, 2)
    scalars = [(x ^ r) * NZ + z for r in rel] + [y ^ r for r in rel] + [c]
    sc = jnp.stack([jnp.asarray(s, jnp.int32) for s in scalars])

    wg, wu, wd = gate_weight[0], up_weight[0], down_weight[0]
    swapped = send(tokens, SWAP)
    swapped, wg, wu = lax.optimization_barrier((swapped, wg, wu))
    message = prepare(sc, tokens, swapped, routes, gate_scales)
    first_pair = (wg, wu, send(wg, SWAP), send(wu, SWAP))
    message, wd = lax.optimization_barrier((message, wd))
    down_pair = (wd, send(wd, SWAP))

    block = {1: send(message, ZIN)}
    rows, wide, hidden, out, home = {}, {}, {}, {}, {}
    gx = GY[GATHER_X]
    gh = GY[GATHER_H]
    lead = ORDER[0]
    early = first_pair[2:] if WEARLY == 0 else ()
    if lead == 2:
        block[2] = send(block[1], ZIN)
    got = dispatch(sc, block[lead], ONWARD, early)
    routed = got[:4]
    onward = got[4] if ONWARD else block[lead]
    for k in range(lead + 1, 4):
        block[k] = send(onward, ZIN)
        onward = block[k]
    block[4] = jnp.where(c == 0, message, send(block[3], ZIN1))
    for i, k in enumerate(ORDER):
        if i > 0:
            before = ORDER[i - 1]
            after = ()
            kind = DEP[i]
            if 'r' in kind:
                after += (rows[before],)
            if 'n' in kind:
                after += (wide[before][0],)
            if 'f' in kind and i > 1:
                after += (wide[ORDER[i - 2]][1],)
            if 'h' in kind and i > 1:
                after += (hidden[ORDER[i - 2]],)
            if i == 1 + WEARLY and WEARLY:
                after += first_pair[2:]
            if i == 1:
                after += down_pair[1:]
            routed = dispatch(sc, block[k], False, after)
        rows[k] = exchange_x(*routed, XIN)
        wide[k] = gx(rows[k])
        after = ()
        if i > 0 and CHAIN:
            after += (hidden[ORDER[i - 1]],)
        if i > LAG:
            after += (out[ORDER[i - 1 - LAG]][0],)
        hidden[k] = gate_up(sc, wide[k], first_pair, after)
        after = (home[ORDER[i - HLAG]],) if i >= HLAG else ()
        out[k] = down(sc, gh(hidden[k]), down_pair, after)
        home[k] = combine(sc, block[k], exchange_x(*out[k], XOUT), (), BF if k == ORDER[3] or END == 0 else F32)
    f4 = home[4].astype(F32)
    if END == 0:
        total = jnp.where(c == 0, home[4], send(home[4], ZOUT[4])).astype(F32)
        for k in (1, 2, 3):
            total = total + send(home[k], ZOUT[k]).astype(F32)
    elif END == 1:
        chain = home[2].astype(F32) + send(home[3].astype(BF), ZOUT[1]).astype(F32)
        chain = home[1].astype(F32) + send(chain.astype(BF), ZOUT[1]).astype(F32)
        total = jnp.where(c == 0, home[4], send(home[4].astype(BF), ZOUT[4]).astype(home[4].dtype)).astype(F32)
        total = total + send(chain.astype(BF), ZOUT[1]).astype(F32)
    elif END == 2:
        chain = home[3].astype(F32) + send(home[4], ZOUT1).astype(F32)
        chain = home[1].astype(F32) + send(chain.astype(BF), ZOUT[2]).astype(F32)
        total = send(chain.astype(BF), ZOUT[1]).astype(F32) + send(home[2].astype(BF), ZOUT[2]).astype(F32)
        total = total + jnp.where(c == 0, f4, 0.0)
    else:
        chain = home[3].astype(F32) + send(home[4], ZOUT1).astype(F32)
        chain = home[2].astype(F32) + send(chain.astype(BF), ZOUT[1]).astype(F32)
        total = send(chain.astype(BF), ZOUT[2]).astype(F32) + send(home[1].astype(BF), ZOUT[1]).astype(F32)
        total = total + jnp.where(c == 0, f4, 0.0)
    return (total[:, :w] + send(total[:, w:], SWAP)).astype(BF)


def solution(mesh):
    in_specs = (
        P("expert", "tensor"),
        P("expert", None),
        P("expert", None),
        P("expert", None, "tensor"),
        P("expert", None, "tensor"),
        P("expert", None, "tensor"),
    )
    return jax.shard_map(
        on_device, mesh=mesh, in_specs=in_specs, out_specs=P("expert", "tensor"), check_vma=False
    )
```

```python
import jax
import jax.numpy as jnp
from jax import lax
from jax.experimental import pallas as pl
from jax.experimental.pallas import tpu as pltpu
from jax.sharding import PartitionSpec as P

NX, NZ, NY, NC = 4, 8, 4, 2
CAP = 40
META = 128
AXES = ("expert", "tensor")
BF = jnp.bfloat16
F32 = jnp.float32
ORDER = (1, 3, 4, 2)
LAG = 1
HLAG = 2
CHAIN = True
SCALE = 1.0
XIN = True
XOUT = True
GATHER_X = 2
GATHER_H = 2
DEP = ('', 'r', 'r', 'r')
ONWARD = True
WEARLY = 0
END = 0


def pairs(move, keep=lambda x, z, y, c: True):
    out = []
    for x in range(NX):
        for z in range(NZ):
            for y in range(NY):
                for c in range(NC):
                    if keep(x, z, y, c):
                        a, b, d, e = move(x, z, y, c)
                        out.append((((x * NZ + z) * NY + y) * NC + c, ((a * NZ + b) * NY + d) * NC + e))
    return out


def first(c):
    return 1 if c == 0 else 3


def second(c):
    return 3 if c == 0 else 1


SWAP = pairs(lambda x, z, y, c: (x, z, y, 1 - c))
XP = pairs(lambda x, z, y, c: (x ^ first(c), z, y, c))
XQ = pairs(lambda x, z, y, c: (x ^ second(c), z, y, c))
YP = pairs(lambda x, z, y, c: (x, z, y ^ first(c), c))
YQ = pairs(lambda x, z, y, c: (x, z, y ^ second(c), c))
X2 = pairs(lambda x, z, y, c: (x ^ 2, z, y, c))
Y2 = pairs(lambda x, z, y, c: (x, z, y ^ 2, c))
ZIN = pairs(lambda x, z, y, c: (x, (z + (2 * c - 1)) % NZ, y, c))
ZIN1 = pairs(lambda x, z, y, c: (x, (z + (2 * c - 1)) % NZ, y, c), lambda x, z, y, c: c == 1)
ZOUT1 = pairs(lambda x, z, y, c: (x, (z - (2 * c - 1)) % NZ, y, c), lambda x, z, y, c: c == 1)
ZOUT = {
    k: pairs(lambda x, z, y, c, k=k: (x, (z + k * (1 - 2 * c)) % NZ, y, c), lambda x, z, y, c, k=k: k < 4 or c == 1)
    for k in (1, 2, 3, 4)
}


def send(value, perm):
    return lax.ppermute(value, AXES, perm)


def vmem(value):
    return pltpu.with_memory_space_constraint(value, pltpu.VMEM)


def call(body, name, out_shape, sc, *args, flops=0, after=()):
    moved = 2 * sum(a.size for a in args)
    spec = pl.BlockSpec(memory_space=pltpu.VMEM)
    count = 1 + len(args)

    def run(*refs):
        body(*refs[:count], *refs[count + len(after) :])

    return pl.pallas_call(
        run,
        name=name,
        out_shape=out_shape,
        in_specs=[pl.BlockSpec(memory_space=pltpu.SMEM)] + [spec] * len(args) + [pl.BlockSpec(memory_space=pl.ANY)] * len(after),
        out_specs=jax.tree.map(lambda _: spec, out_shape),
        compiler_params=pltpu.CompilerParams(vmem_limit_bytes=16 * 1024 * 1024),
        cost_estimate=pl.CostEstimate(flops=int(flops * SCALE), bytes_accessed=int(moved * SCALE), transcendentals=0),
    )(sc, *[vmem(a) for a in args], *after)


def iota(shape, dim):
    return lax.broadcasted_iota(jnp.int32, shape, dim)


def prepare_body(sc, own, other, routes, scales, out):
    n = own.shape[0]
    lane = iota((n, META), 1)
    expert = lax.rem(lane, 32)
    group = lax.div(lane, 32)
    chosen = jnp.zeros((n, META), F32)
    scale = jnp.zeros((n, META), F32)
    for k in range(routes.shape[1]):
        hit = routes[:, k : k + 1] == expert
        chosen = chosen + jnp.where(hit, 1.0, 0.0)
        scale = scale + jnp.where(hit, scales[:, k : k + 1], 0.0)
    earlier = jnp.where(iota((n, n), 1) < iota((n, n), 0), 1.0, 0.0).astype(BF)
    slot = jnp.dot(earlier, chosen.astype(BF), preferred_element_type=F32)
    slot = jnp.where(chosen > 0.0, slot, -1.0)
    high = scale.astype(BF).astype(F32)
    low = scale - high
    meta = jnp.where(group == 0, slot, jnp.where(group == 1, high, jnp.where(group == 2, low, 0.0)))
    w = own.shape[1]
    out[:, 2 * w :] = meta.astype(BF)
    for core in range(NC):

        @pl.when(sc[8] == core)
        def _(core=core):
            out[:, core * w : (core + 1) * w] = own[...]
            out[:, (1 - core) * w : (2 - core) * w] = other[...]


def prepare(sc, own, other, routes, scales):
    n, w = own.shape
    shape = jax.ShapeDtypeStruct((n, 2 * w + META), BF)
    return call(prepare_body, "prepare", shape, sc, own, other, routes, scales, flops=2 * n * n * META)


def row_pick(rows, experts, base):
    r = iota((rows, META), 0)
    col = iota((rows, META), 1)
    want = jnp.full((rows, META), -1, jnp.int32)
    for i, e in enumerate(experts):
        want = jnp.where((r >= i * CAP) & (r < (i + 1) * CAP), e + base, want)
    return jnp.where(col == want, 1.0, 0.0).astype(BF)


def nt(a, b):
    return lax.dot_general(a, b, (((1,), (1,)), ((), ())), preferred_element_type=F32)


def dispatch_body(sc, msg, *outs):
    w = outs[0].shape[1]
    n = msg.shape[0]
    rows = 4 * CAP
    pos = nt(row_pick(rows, [sc[j] for j in range(4)], 0), msg[:, w:])
    slot = lax.rem(iota((rows, n), 0), CAP).astype(F32)
    table = jnp.where(pos == slot, 1.0, 0.0).astype(BF)
    picked = jnp.dot(table, msg[:, :w], preferred_element_type=F32)
    for j in range(4):
        outs[j][...] = picked[j * CAP : (j + 1) * CAP].astype(BF)
    if len(outs) == 5:
        outs[4][...] = msg[...]


def dispatch(sc, msg, onward, after=()):
    n, full = msg.shape
    w = full - META
    shapes = [jax.ShapeDtypeStruct((CAP, w), BF)] * 4
    if onward:
        shapes = shapes + [jax.ShapeDtypeStruct(msg.shape, BF)]
    return call(dispatch_body, "dispatch", shapes, sc, msg, flops=8 * CAP * n * w, after=after)


def matmul(pieces, weight, sc):
    total = None
    for s in range(4):
        pair = pieces[s // 2]
        n, k = pair.shape[0] // 2, pair.shape[1]
        rows = pl.ds(pl.multiple_of(sc[4 + s] * k, 256), k)
        x = pair[s % 2 * n : (s % 2 + 1) * n, :]
        part = jnp.dot(x, weight[rows, :], preferred_element_type=F32)
        total = part if total is None else total + part
    return total


def gate_up_body(sc, near, far, g_own, u_own, g_other, u_other, out):
    n = g_own.shape[1]
    halves = []
    for gw, uw in ((g_own, u_own), (g_other, u_other)):
        v = matmul((near, far), gw, sc)
        u = matmul((near, far), uw, sc)
        halves.append((v / (1.0 + jnp.exp(-v)) * u).astype(BF))
    for core in range(NC):

        @pl.when(sc[8] == core)
        def _(core=core):
            out[:, core * n : (core + 1) * n] = halves[0]
            out[:, (1 - core) * n : (2 - core) * n] = halves[1]


def gate_up(sc, pieces, weights, after=()):
    rows, w = pieces[0].shape[0] // 2, pieces[0].shape[1]
    n = weights[0].shape[1]
    shape = jax.ShapeDtypeStruct((rows, 2 * n), BF)
    return call(gate_up_body, "gate_up", shape, sc, *pieces, *weights, flops=2 * rows * 4 * w * 4 * n, after=after)


def down_body(sc, near, far, d_own, d_other, *outs):
    n = d_own.shape[1]
    for i, w in enumerate((d_own, d_other)):
        total = matmul((near, far), w, sc)
        for j in range(4):
            outs[j][:, i * n : (i + 1) * n] = total[j * CAP : (j + 1) * CAP].astype(BF)


def down(sc, pieces, weights, after=()):
    rows, w = pieces[0].shape[0] // 2, pieces[0].shape[1]
    n = weights[0].shape[1]
    shapes = [jax.ShapeDtypeStruct((CAP, 2 * n), BF)] * 4
    return call(down_body, "down", shapes, sc, *pieces, *weights, flops=2 * rows * 4 * w * 2 * n, after=after)


def combine_body(sc, msg, rows_ref, *rest):
    out = rest[-1]
    w = out.shape[1]
    meta = msg[:, w:]
    n = meta.shape[0]
    rows = rows_ref.shape[0]
    experts = [sc[j] for j in range(4)]
    here = nt(meta, row_pick(rows, experts, 0)) == lax.rem(iota((n, rows), 1), CAP).astype(F32)
    weight = [jnp.where(here, nt(meta, row_pick(rows, experts, base)), 0.0) for base in (32, 64)]
    part = jnp.dot(jnp.concatenate(weight, axis=0).astype(BF), rows_ref[...], preferred_element_type=F32)
    total = part[:n] + part[n:]
    for ref in rest[:-1]:
        total = total + ref[...].astype(F32)
    out[...] = total.astype(out.dtype)


def combine(sc, msg, rows, acc, dtype):
    n = msg.shape[0]
    w = rows.shape[1]
    shape = jax.ShapeDtypeStruct((n, w), dtype)
    return call(combine_body, "combine", shape, sc, msg, rows, *acc, flops=4 * n * w * 4 * CAP)


def gather_y(value):
    pair = jnp.concatenate([value, send(value, YP)], axis=0)
    return pair, send(pair, YQ)


def exchange_x(own, p, q, two, direct):
    if direct:
        return jnp.concatenate([own, send(p, XP), send(q, XQ), send(two, X2)], axis=0)
    got = send(jnp.concatenate([p, two], axis=0), XP)
    got2 = send(jnp.concatenate([q, got[CAP:]], axis=0), XQ)
    return jnp.concatenate([own, got[:CAP], got2], axis=0)


def gather_three(value):
    one = send(value, YP)
    two = send(value, YQ)
    return jnp.concatenate([value, one], axis=0), jnp.concatenate([two, send(one, YQ)], axis=0)


def gather_direct(value):
    one = send(value, YP)
    two = send(value, YQ)
    return jnp.concatenate([value, one], axis=0), jnp.concatenate([two, send(value, Y2)], axis=0)


GY = {2: gather_y, 3: gather_three, 1: gather_direct}


def on_device(tokens, routes, gate_scales, gate_weight, up_weight, down_weight):
    w = tokens.shape[1]
    expert = lax.axis_index("expert")
    tensor = lax.axis_index("tensor")
    x, z = expert // NZ, expert % NZ
    y, c = tensor // NC, tensor % NC
    rel = (0, 1 + 2 * c, 3 - 2 * c, 2)
    scalars = [(x ^ r) * NZ + z for r in rel] + [y ^ r for r in rel] + [c]
    sc = jnp.stack([jnp.asarray(s, jnp.int32) for s in scalars])

    wg, wu, wd = gate_weight[0], up_weight[0], down_weight[0]
    swapped = send(tokens, SWAP)
    swapped, wg, wu = lax.optimization_barrier((swapped, wg, wu))
    message = prepare(sc, tokens, swapped, routes, gate_scales)
    first_pair = (wg, wu, send(wg, SWAP), send(wu, SWAP))
    message, wd = lax.optimization_barrier((message, wd))
    down_pair = (wd, send(wd, SWAP))

    block = {1: send(message, ZIN)}
    rows, wide, hidden, out, home = {}, {}, {}, {}, {}
    gx = GY[GATHER_X]
    gh = GY[GATHER_H]
    lead = ORDER[0]
    early = first_pair[2:] if WEARLY == 0 else ()
    if lead == 2:
        block[2] = send(block[1], ZIN)
    got = dispatch(sc, block[lead], ONWARD, early)
    routed = got[:4]
    onward = got[4] if ONWARD else block[lead]
    for k in range(lead + 1, 4):
        block[k] = send(onward, ZIN)
        onward = block[k]
    block[4] = jnp.where(c == 0, message, send(block[3], ZIN1))
    for i, k in enumerate(ORDER):
        if i > 0:
            before = ORDER[i - 1]
            after = ()
            kind = DEP[i]
            if 'r' in kind:
                after += (rows[before],)
            if 'n' in kind:
                after += (wide[before][0],)
            if 'f' in kind and i > 1:
                after += (wide[ORDER[i - 2]][1],)
            if 'h' in kind and i > 1:
                after += (hidden[ORDER[i - 2]],)
            if i == 1 + WEARLY and WEARLY:
                after += first_pair[2:]
            if i == 1:
                after += down_pair[1:]
            routed = dispatch(sc, block[k], False, after)
        rows[k] = exchange_x(*routed, XIN)
        wide[k] = gx(rows[k])
        after = ()
        if i > 0 and CHAIN:
            after += (hidden[ORDER[i - 1]],)
        if i > LAG:
            after += (out[ORDER[i - 1 - LAG]][0],)
        hidden[k] = gate_up(sc, wide[k], first_pair, after)
        after = (home[ORDER[i - HLAG]],) if i >= HLAG else ()
        out[k] = down(sc, gh(hidden[k]), down_pair, after)
        home[k] = combine(sc, block[k], exchange_x(*out[k], XOUT), (), BF if k == ORDER[3] or END == 0 else F32)
    f4 = home[4].astype(F32)
    if END == 0:
        total = jnp.where(c == 0, home[4], send(home[4], ZOUT[4])).astype(F32)
        for k in (1, 2, 3):
            total = total + send(home[k], ZOUT[k]).astype(F32)
    elif END == 1:
        chain = home[2].astype(F32) + send(home[3].astype(BF), ZOUT[1]).astype(F32)
        chain = home[1].astype(F32) + send(chain.astype(BF), ZOUT[1]).astype(F32)
        total = jnp.where(c == 0, home[4], send(home[4].astype(BF), ZOUT[4]).astype(home[4].dtype)).astype(F32)
        total = total + send(chain.astype(BF), ZOUT[1]).astype(F32)
    elif END == 2:
        chain = home[3].astype(F32) + send(home[4], ZOUT1).astype(F32)
        chain = home[1].astype(F32) + send(chain.astype(BF), ZOUT[2]).astype(F32)
        total = send(chain.astype(BF), ZOUT[1]).astype(F32) + send(home[2].astype(BF), ZOUT[2]).astype(F32)
        total = total + jnp.where(c == 0, f4, 0.0)
    else:
        chain = home[3].astype(F32) + send(home[4], ZOUT1).astype(F32)
        chain = home[2].astype(F32) + send(chain.astype(BF), ZOUT[1]).astype(F32)
        total = send(chain.astype(BF), ZOUT[2]).astype(F32) + send(home[1].astype(BF), ZOUT[1]).astype(F32)
        total = total + jnp.where(c == 0, f4, 0.0)
    return (total[:, :w] + send(total[:, w:], SWAP)).astype(BF)


def solution(mesh):
    in_specs = (
        P("expert", "tensor"),
        P("expert", None),
        P("expert", None),
        P("expert", None, "tensor"),
        P("expert", None, "tensor"),
        P("expert", None, "tensor"),
    )
    return jax.shard_map(
        on_device, mesh=mesh, in_specs=in_specs, out_specs=P("expert", "tensor"), check_vma=False
    )
```
